512 devices in a mesh: ctx: 64 (over z, y_lo, core), tp: 8 (over x, y_hi).
Axes of the slice: x: 4, y: 4 (y_hi: 2, y_lo: 2; y = y_hi * 2 + y_lo), z: 16, core: 2. Of those that a mesh axis runs over, the one named last changes fastest.
Arguments:
- queries: bfloat16 [65536, 1024], P('ctx', 'tp'), may hold values from -6 to 6
- audio_keys: bfloat16 [2048, 1024], P('ctx', 'tp'), may hold values from -6 to 6
- audio_values: bfloat16 [2048, 1024], P('ctx', 'tp'), may hold values from -6 to 6
- grad_output: bfloat16 [65536, 1024], P('ctx', 'tp'), may hold values from -6 to 6
- out_weight: bfloat16 [1024, 1024], P('tp'), may hold values from -0.1875 to 0.1875
Outputs:
- grad_queries: bfloat16 [65536, 1024], P('ctx', 'tp')
- grad_keys: bfloat16 [2048, 1024], P('ctx', 'tp')
- grad_values: bfloat16 [2048, 1024], P('ctx', 'tp')
- grad_weight: float32 [1024, 1024], P('tp', 'ctx')
The draws below stay inside these ranges and needn't reach their ends.
All inputs are finite; a program needn't handle non-finite values.
Results may differ from the reference program's by a relative error of at most 0.033.
Values may be sent and summed in bfloat16 or wider, within the bound.
A program may use at most 64 MiB of HBM per device.

```python
import math
import jax
import jax.numpy as jnp
from jax import lax

D = 1024
HEADS = 8
HD = 128
VIDEO = 65536
AUDIO = 2048


def draw_queries(key, part):
    key = jax.random.fold_in(key, 5)
    base = jnp.clip(1.4 * jax.random.normal(key, (VIDEO, D), jnp.float32), -6.0, 6.0)
    return base.astype(jnp.bfloat16)


def draw_audio_keys(key, part):
    key = jax.random.fold_in(key, 9)
    base = jnp.clip(1.4 * jax.random.normal(key, (AUDIO, D), jnp.float32), -6.0, 6.0)
    return base.astype(jnp.bfloat16)


def level_of(rng, shape, shards, low, top_value):
    def one(position, blocks):
        steps = jax.random.uniform(jax.random.fold_in(jax.random.fold_in(rng, 6), position), (blocks,), jnp.float32, low / len(shards), top_value / len(shards))
        return jnp.repeat(jnp.exp(steps), shape[position] // blocks).reshape((-1,) + (1,) * (len(shape) - position - 1))

    level = one(*shards[0])
    for cut in shards[1:]:
        level = level * one(*cut)
    return level


def centred(rng, dims, spread, most, cuts=(), kind=jnp.bfloat16):
    result = spread * jax.random.normal(rng, dims, jnp.float32)
    if cuts:
        result = result * level_of(rng, dims, cuts, -0.22, 0.18)
    return jnp.clip(result, -most, most).astype(kind)


def setup_inputs(seed: int = 0) -> dict:
    splits = jax.random.split(jax.random.key(seed), 6)
    return {
        "queries": draw_queries(jax.random.fold_in(splits[5], 71), 0),
        "audio_keys": draw_audio_keys(jax.random.fold_in(splits[5], 71), 0),
        "audio_values": centred(splits[2], (AUDIO, D), 1.0, 6.0, ((0, 64), (1, 8))),
        "grad_output": centred(splits[3], (VIDEO, D), 1.0, 6.0, ((0, 64), (1, 8))),
        "out_weight": centred(splits[4], (D, D), D ** -0.5, 0.1875, ((0, 8),)),
    }


def head_pass(operands):
    query_head, key_head, value_head, grad_head = operands
    factor = 1.0 / math.sqrt(HD)
    block_rows = min(VIDEO, 4096)

    def advance(carried, counter):
        key_grad, value_grad = carried
        query_block = lax.dynamic_slice_in_dim(query_head, counter * block_rows, block_rows, 0)
        grad_block = lax.dynamic_slice_in_dim(grad_head, counter * block_rows, block_rows, 0)
        scores = jnp.dot(query_block, key_head.T, preferred_element_type=jnp.float32) * factor
        row_max = lax.optimization_barrier(jnp.max(scores, axis=1, keepdims=True))
        logsum = row_max + jnp.log(lax.optimization_barrier(jnp.sum(jnp.exp(scores - row_max), axis=1, keepdims=True)))
        probs = jnp.exp(scores - logsum).astype(jnp.bfloat16)
        attended = jnp.dot(probs, value_head, preferred_element_type=jnp.float32).astype(jnp.bfloat16)
        row_delta = lax.optimization_barrier(jnp.sum(grad_block.astype(jnp.float32) * attended.astype(jnp.float32), axis=1, keepdims=True))
        grad_probs = jnp.dot(grad_block, value_head.T, preferred_element_type=jnp.float32)
        grad_scores = (probs.astype(jnp.float32) * (grad_probs - row_delta)).astype(jnp.bfloat16)
        query_grad = (jnp.dot(grad_scores, key_head, preferred_element_type=jnp.float32) * factor).astype(jnp.bfloat16)
        key_grad = key_grad + jnp.dot(grad_scores.T, query_block, preferred_element_type=jnp.float32) * factor
        value_grad = value_grad + jnp.dot(probs.T, grad_block, preferred_element_type=jnp.float32)
        return ((key_grad, value_grad), (attended, query_grad))
    zeros = jnp.zeros((AUDIO, HD), jnp.float32)
    (key_grad, value_grad), (attended, query_grad) = lax.scan(advance, (zeros, zeros), jnp.arange(VIDEO // block_rows, dtype=jnp.int32))
    return (attended.reshape(VIDEO, HD), query_grad.reshape(VIDEO, HD), key_grad.astype(jnp.bfloat16), value_grad.astype(jnp.bfloat16))

def by_heads(matrix, rows_total):
    return jnp.transpose(matrix.reshape(rows_total, HEADS, HD), (1, 0, 2))

def from_heads(stacked, rows_total):
    return jnp.transpose(stacked, (1, 0, 2)).reshape(rows_total, D)

def reference(queries, audio_keys, audio_values, grad_output, out_weight):
    grad_attended = jnp.dot(grad_output, out_weight.T, preferred_element_type=jnp.float32).astype(jnp.bfloat16)
    attended, query_grad, key_grad, value_grad = lax.map(head_pass, (by_heads(queries, VIDEO), by_heads(audio_keys, AUDIO), by_heads(audio_values, AUDIO), by_heads(grad_attended, VIDEO)))
    attended_full = from_heads(attended, VIDEO)
    grad_weight = jnp.dot(attended_full.T, grad_output, preferred_element_type=jnp.float32)
    return (from_heads(query_grad, VIDEO), from_heads(key_grad, AUDIO), from_heads(value_grad, AUDIO), grad_weight)
```

```python
import functools
import math

import jax
import jax.numpy as jnp
from jax import lax
from jax.experimental import pallas as pl
from jax.experimental.pallas import tpu as pltpu
from jax.sharding import PartitionSpec as P

MESH = pl.DeviceIdType.MESH
F32, BF16 = jnp.float32, jnp.bfloat16
HD = 128
ROWS = 1024
GROUP = 512
PARTS = 4
PART = ROWS // PARTS
FACTOR = 1.0 / math.sqrt(HD)
LOG2E = math.log2(math.e)
OFFSETS = (2, 1, 3, 0)
TP_SHIFTS = tuple((a, b) for a in range(4) for b in range(2) if a or b)


def nn(a, b):
    return lax.dot_general(a, b, (((1,), (0,)), ((), ())), preferred_element_type=F32)


def nt(a, b):
    return lax.dot_general(a, b, (((1,), (1,)), ((), ())), preferred_element_type=F32)


def tn(a, b):
    return lax.dot_general(a, b, (((0,), (0,)), ((), ())), preferred_element_type=F32)


def kernel(
    q_ref, k_ref, v_ref, g_ref, w_ref,
    dq_ref, dk_ref, dv_ref, dw_ref,
    kv, gall, scores, probs, att_t, da_t, da, dq_t, acc, keep,
    s1, r1, s2, r2, s3, r3, s4, r4, tot,
    za_s, za_r, zb_s, zb_r, ya_s, ya_r, ca_s, ca_r, g_s, g_r,
    c1_s, c1_r, y2_s, y2_r, z3_s, z3_r, z4_s, z4_r,
):
    ctx, tp = lax.axis_index("ctx"), lax.axis_index("tp")
    z, yl, core = ctx // 4, (ctx // 2) % 2, ctx % 2
    zh, zl = z // 4, z % 4

    def on_ctx(dz=0, dy=0, dc=0):
        there = ((z + dz) % 16) * 4 + ((yl + dy) % 2) * 2 + (core + dc) % 2
        return (there, tp)

    def on_tp(dx, dy):
        return (ctx, ((tp // 2 + dx) % 4) * 2 + (tp % 2 + dy) % 2)

    def copy(src, dst, ssem, rsem, to):
        return pltpu.make_async_remote_copy(
            src_ref=src, dst_ref=dst, send_sem=ssem, recv_sem=rsem, device_id=to, device_id_type=MESH
        )

    barrier = pltpu.get_barrier_semaphore()
    greeted = [on_ctx(dc=1), on_ctx(dy=1)]
    greeted += [on_ctx(dz=d) for d in (1, 15, 2, 14, 4, 8, 12)]
    greeted += [on_tp(*d) for d in TP_SHIFTS]
    for there in greeted:
        pl.semaphore_signal(barrier, inc=1, device_id=there, device_id_type=MESH)
    kv[zl, 0, core, yl, pl.ds(zh * 32, 32)] = k_ref[...]
    kv[zl, 1, core, yl, pl.ds(zh * 32, 32)] = v_ref[...]
    gall[tp] = g_ref[...]
    pl.semaphore_wait(barrier, len(greeted))

    sends = []

    def go(c):
        c.start()
        sends.append(c)
        return c

    own = kv.at[zl, :, core, yl, pl.ds(zh * 32, 32)]
    far = [
        go(copy(own, own, za_s.at[i], za_r.at[i], on_ctx(dz=4 * (i + 1)))) for i in range(3)
    ]
    gcopies = {}

    def send_grad(part):
        rows = pl.ds(part * PART, PART)
        for i, d in enumerate(TP_SHIFTS):
            gcopies[i, part] = go(
                copy(g_ref.at[rows], gall.at[tp, rows], g_s.at[i, part], g_r.at[i, part], on_tp(*d))
            )

    send_grad(0)
    send_grad(1)
    for c in far:
        c.wait_recv()
    piece = kv.at[zl, :, core, yl]
    near = [
        go(copy(piece, piece, zb_s.at[i], zb_r.at[i], on_ctx(dz=d))) for i, d in enumerate((2, 1, 15))
    ]
    order = ((zl, None), ((zl + 3) % 4, 1), ((zl + 1) % 4, 2), ((zl + 2) % 4, 0))
    across, swap = [], []
    for i, (r, src) in enumerate(order):
        if src is not None:
            near[src].wait_recv()
        p = kv.at[r, :, core, yl]
        across.append(go(copy(p, p, ya_s.at[i], ya_r.at[i], on_ctx(dy=1))))
        if i == 0:
            send_grad(2)
            send_grad(3)
    for i, (r, _) in enumerate(order):
        across[i].wait_recv()
        p = kv.at[r, :, core]
        swap.append(go(copy(p, p, ca_s.at[i], ca_r.at[i], on_ctx(dc=1))))

    top = jnp.full((8, ROWS), -jnp.inf, F32)
    for i, (r, _) in enumerate(order):
        swap[i].wait_recv()
        for h in range(2):
            kb = kv[r, 0, h].reshape(256, HD)
            s = nt(kb, q_ref[...])
            scores[i, pl.ds(h * 256, 256)] = s
            top = jnp.maximum(top, jnp.max(s.reshape(32, 8, ROWS), axis=0))
    shift = jnp.max(top, axis=0, keepdims=True) * (FACTOR * LOG2E)
    total = jnp.zeros((8, ROWS), F32)
    acc_t = jnp.zeros((HD, ROWS), F32)
    for i, (r, _) in enumerate(order):
        for h in range(2):
            vb = kv[r, 1, h].reshape(256, HD)
            e = jnp.exp2(scores[i, pl.ds(h * 256, 256)] * (FACTOR * LOG2E) - shift)
            total = total + jnp.sum(e.reshape(32, 8, ROWS), axis=0)
            eb = e.astype(BF16)
            probs[i, pl.ds(h * 256, 256)] = eb
            acc_t = acc_t + tn(vb, eb)
    inverse = 1.0 / jnp.sum(total, axis=0, keepdims=True)
    att_t[...] = (acc_t * inverse).astype(BF16)

    for part in range(PARTS):
        for i in range(len(TP_SHIFTS)):
            gcopies[i, part].wait_recv()
    x_t = jnp.zeros((HD, ROWS), F32)
    for b in range(8):
        x_t = x_t + nt(w_ref[:, b * 128 : (b + 1) * 128], gall[b])
    x_t = x_t * inverse
    delta = jnp.sum(x_t * att_t[...].astype(F32), axis=0, keepdims=True)
    da_t[...] = x_t.astype(BF16)
    da[...] = x_t.T.astype(BF16)

    for b in range(8):
        part_w = nn(att_t[...], gall[b]).T
        for j in range(8):
            zz, o = 2 * b + j // 4, j % 4
            g = (zz % 4 - zl + 4) % 4
            slot = jnp.where(g == 2, 0, jnp.where(g == 1, 1, jnp.where(g == 3, 2, 3)))
            acc[slot, o % 2, o // 2, pl.ds(256 + (zz // 4) * 16, 16)] = part_w[j * 16 : (j + 1) * 16]

    position = {2: 3, 1: 2, 3: 1, 0: 0}
    dq_t[...] = jnp.zeros((HD, ROWS), F32)
    first, second, third = [None] * 4, [None] * 4, [None] * 3

    def compute(g):
        r = (zl + OFFSETS[g]) % 4
        i = position[OFFSETS[g]]
        for h in range(2):
            kb = kv[r, 0, h].reshape(256, HD)
            vb = kv[r, 1, h].reshape(256, HD)
            pb = probs[i, pl.ds(h * 256, 256)]
            ds = (pb.astype(F32) * (nn(vb, da_t[...]) - delta)).astype(BF16)
            acc[g, h, :, pl.ds(0, 128)] = (nn(ds, q_ref[...]) * FACTOR).reshape(2, 128, HD)
            acc[g, h, :, pl.ds(128, 128)] = nn(pb, da[...]).reshape(2, 128, HD)
            dq_t[...] += tn(kb, ds)
        s1[g] = acc[g, 1 - core].astype(BF16)
        first[g] = go(copy(s1.at[g], r1.at[g], c1_s.at[g], c1_r.at[g], on_ctx(dc=1)))

    def step_y(g):
        first[g].wait_recv()
        s2[g] = (acc[g, core, 1 - yl] + r1[g, 1 - yl].astype(F32)).astype(BF16)
        second[g] = go(copy(s2.at[g], r2.at[g], y2_s.at[g], y2_r.at[g], on_ctx(dy=1)))
        keep[g] = acc[g, core, yl] + r1[g, yl].astype(F32)

    def step_z(g):
        second[g].wait_recv()
        if g == 3:
            tot[...] = keep[g] + r2[g].astype(F32)
        else:
            s3[g] = (keep[g] + r2[g].astype(F32)).astype(BF16)
            there = on_ctx(dz=(2, 1, 15)[g])
            third[g] = go(copy(s3.at[g], r3.at[g], z3_s.at[g], z3_r.at[g], there))

    for g in range(4):
        compute(g)
        if g >= 1:
            step_y(g - 1)
        if g >= 2:
            step_z(g - 2)
    step_y(3)
    step_z(2)
    dq_ref[...] = (dq_t[...] * FACTOR).T.astype(BF16)
    step_z(3)
    for c in third:
        c.wait_recv()
    tot[...] += (r3[0].astype(F32) + r3[1].astype(F32)) + r3[2].astype(F32)

    def cut(h):
        return (
            tot[pl.ds(h * 32, 32)],
            tot[pl.ds(128 + h * 32, 32)],
            tot[pl.ds(256 + h * 16, 16)],
        )

    last = []
    for i in range(3):
        a, b, c = cut((zh + i + 1) % 4)
        s4[i, 0:32] = a.astype(BF16)
        s4[i, 32:64] = b.astype(BF16)
        s4[i, 64:80] = c.astype(BF16)
        last.append(
            go(copy(s4.at[i], r4.at[i], z4_s.at[i], z4_r.at[i], on_ctx(dz=4 * (i + 1))))
        )
    a, b, c = cut(zh)
    for copy_in in last:
        copy_in.wait_recv()
    more = (r4[0].astype(F32) + r4[1].astype(F32)) + r4[2].astype(F32)
    dk_ref[...] = (a + more[0:32]).astype(BF16)
    dv_ref[...] = (b + more[32:64]).astype(BF16)
    dw_ref[...] = c + more[64:80]
    for c in sends:
        c.wait_send()


def local(queries, audio_keys, audio_values, grad_output, out_weight):
    vmem = pl.BlockSpec(memory_space=pltpu.VMEM)
    dma = lambda *n: pltpu.SemaphoreType.DMA(n)
    scratch = [
        pltpu.VMEM((4, 2, 2, 2, 128, HD), BF16),
        pltpu.VMEM((8, ROWS, 128), BF16),
        pltpu.VMEM((4, GROUP, ROWS), F32),
        pltpu.VMEM((4, GROUP, ROWS), BF16),
        pltpu.VMEM((HD, ROWS), BF16),
        pltpu.VMEM((HD, ROWS), BF16),
        pltpu.VMEM((ROWS, HD), BF16),
        pltpu.VMEM((HD, ROWS), F32),
        pltpu.VMEM((4, 2, 2, 320, HD), F32),
        pltpu.VMEM((4, 320, HD), F32),
        pltpu.VMEM((4, 2, 320, HD), BF16),
        pltpu.VMEM((4, 2, 320, HD), BF16),
        pltpu.VMEM((4, 320, HD), BF16),
        pltpu.VMEM((4, 320, HD), BF16),
        pltpu.VMEM((3, 320, HD), BF16),
        pltpu.VMEM((3, 320, HD), BF16),
        pltpu.VMEM((3, 80, HD), BF16),
        pltpu.VMEM((3, 80, HD), BF16),
        pltpu.VMEM((320, HD), F32),
        dma(3), dma(3), dma(3), dma(3), dma(4), dma(4), dma(4), dma(4), dma(7, PARTS), dma(7, PARTS),
        dma(4), dma(4), dma(4), dma(4), dma(3), dma(3), dma(3), dma(3),
    ]
    dq, dk, dv, dw = pl.pallas_call(
        kernel,
        out_shape=(
            jax.ShapeDtypeStruct((ROWS, HD), BF16),
            jax.ShapeDtypeStruct((32, HD), BF16),
            jax.ShapeDtypeStruct((32, HD), BF16),
            jax.ShapeDtypeStruct((16, HD), F32),
        ),
        in_specs=[vmem] * 5,
        out_specs=(vmem,) * 4,
        scratch_shapes=scratch,
        compiler_params=pltpu.CompilerParams(
            collective_id=0, has_side_effects=True, vmem_limit_bytes=48 * 2**20
        ),
    )(queries, audio_keys, audio_values, grad_output, out_weight)
    return dq, dk, dv, dw.T


def solution(mesh):
    return jax.shard_map(
        local,
        mesh=mesh,
        in_specs=(P("ctx", "tp"), P("ctx", "tp"), P("ctx", "tp"), P("ctx", "tp"), P("tp", None)),
        out_specs=(P("ctx", "tp"), P("ctx", "tp"), P("ctx", "tp"), P("tp", "ctx")),
        check_vma=False,
    )
```

```python
import math

import jax
import jax.numpy as jnp
from jax import lax
from jax.experimental import pallas as pl
from jax.experimental.pallas import tpu as pltpu
from jax.sharding import PartitionSpec as P

MESH = pl.DeviceIdType.MESH
F32, BF16 = jnp.float32, jnp.bfloat16
HD = 128
ROWS = 1024
CHUNK = 512
KEYS = 32
SLOT = 80
PARTS = 4
PART = ROWS // PARTS
FACTOR = 1.0 / math.sqrt(HD)
LOG2E = math.log2(math.e)
NEAR = (0, 1, 2, 15)
FORTH = (0, 1, 3, 2)
BACK = (2, 1, 3, 0)
SPOTS = [(e, i) for i in (2, 1, 3, 0) for e in range(2) if i or e]


def nn(a, b):
    return lax.dot_general(a, b, (((1,), (0,)), ((), ())), preferred_element_type=F32)


def nt(a, b):
    return lax.dot_general(a, b, (((1,), (1,)), ((), ())), preferred_element_type=F32)


def tn(a, b):
    return lax.dot_general(a, b, (((0,), (0,)), ((), ())), preferred_element_type=F32)


def kernel(
    q_hbm, k_hbm, v_hbm, g_hbm, w_hbm,
    dq_ref, dk_ref, dv_ref, dw_ref,
    q_ref, w_ref, kv, gall, scores, probs, att_t, da_t, da, dq_t, acc,
    s1, r1, s3, r3, s4, r4,
    in_s, far_s, far_r, near_s, near_r, ca_s, ca_r, g_s, g_r,
    c1_s, c1_r, m_s, m_r, z4_s, z4_r,
):
    ctx, tp = lax.axis_index("ctx"), lax.axis_index("tp")
    z, yl, core = ctx // 4, (ctx // 2) % 2, ctx % 2

    def on_ctx(dz=0, dy=0, dc=0):
        there = ((z + dz) % 16) * 4 + ((yl + dy) % 2) * 2 + (core + dc) % 2
        return (there, tp)

    def on_tp(dx, dy):
        return (ctx, ((tp // 2 + dx) % 4) * 2 + (tp % 2 + dy) % 2)

    def copy(src, dst, ssem, rsem, to):
        return pltpu.make_async_remote_copy(
            src_ref=src, dst_ref=dst, send_sem=ssem, recv_sem=rsem, device_id=to, device_id_type=MESH
        )

    own = kv.at[0, :, 0, 0, 0]
    loads = [
        pltpu.make_async_copy(k_hbm, own.at[0], in_s.at[0]),
        pltpu.make_async_copy(v_hbm, own.at[1], in_s.at[1]),
        pltpu.make_async_copy(g_hbm, gall.at[tp], in_s.at[2]),
        pltpu.make_async_copy(q_hbm, q_ref, in_s.at[3]),
        pltpu.make_async_copy(w_hbm, w_ref, in_s.at[4]),
    ]
    for c in loads:
        c.start()
    barrier = pltpu.get_barrier_semaphore()
    greeted = [on_ctx(dc=1), on_ctx(dy=1)]
    greeted += [on_ctx(dz=d, dy=e) for d in (1, 15, 2, 14) for e in range(2)]
    greeted += [on_ctx(dz=d) for d in (4, 8, 12)]
    greeted += [on_tp(0, 1), on_tp(1, 0), on_tp(3, 0)]
    for there in greeted:
        pl.semaphore_signal(barrier, inc=1, device_id=there, device_id_type=MESH)
    for c in loads:
        c.wait()
    pl.semaphore_wait(barrier, len(greeted))

    sends = []

    def go(c):
        c.start()
        sends.append(c)
        return c

    far = {
        k: go(copy(own, kv.at[k, :, 0, 0, 0], far_s.at[k], far_r.at[k], on_ctx(dz=4 * k)))
        for k in (2, 1, 3)
    }
    near = {}

    def send_near(k):
        if k:
            far[k].wait_recv()
        for e, i in SPOTS:
            near[k, e, i] = go(
                copy(
                    kv.at[k, :, 0, 0, 0],
                    kv.at[k, :, 0, e, i],
                    near_s.at[k, e, i],
                    near_r.at[k, e, i],
                    on_ctx(dz=NEAR[i], dy=e),
                )
            )

    swap = {}

    def send_swap(k):
        for e, i in SPOTS:
            near[k, e, i].wait_recv()
        swap[k] = go(copy(kv.at[k, :, 0], kv.at[k, :, 1], ca_s.at[k], ca_r.at[k], on_ctx(dc=1)))

    send_near(0)

    gc = {}

    def send_grad(i, part, dx_from, dy_from, dx, dy):
        rows = pl.ds(part * PART, PART)
        b = gall.at[((tp // 2 + dx_from) % 4) * 2 + (tp % 2 + dy_from) % 2, rows]
        gc[i, part] = go(copy(b, b, g_s.at[i, part], g_r.at[i, part], on_tp(dx, dy)))

    waited = set()

    def arrived(i, part):
        if (i, part) not in waited:
            gc[i, part].wait_recv()
            waited.add((i, part))

    def relay_y(part):
        arrived(0, part)
        send_grad(3, part, 0, 1, 1, 0)
        send_grad(4, part, 0, 1, 3, 0)

    def relay_x(part, dy):
        if part % 2 == 0:
            arrived(1 + 2 * dy, part)
            send_grad(5 + dy, part, 3, dy, 1, 0)
        else:
            arrived(2 + 2 * dy, part)
            send_grad(5 + dy, part, 1, dy, 3, 0)

    def relay_late(part):
        arrived(1, part)
        send_grad(3, part, 3, 0, 0, 1)
        arrived(2, part)
        send_grad(4, part, 1, 0, 0, 1)

    def relay_last(part):
        arrived(5, part)
        send_grad(6, part, 2, 0, 0, 1)

    for part in range(PARTS):
        send_grad(0, part, 0, 0, 0, 1)
        send_grad(1, part, 0, 0, 1, 0)
        send_grad(2, part, 0, 0, 3, 0)
    relay_y(0)
    send_near(1)
    send_near(3)
    relay_y(1)
    relay_x(0, 0)
    relay_y(2)
    relay_x(1, 0)
    send_near(2)
    relay_x(2, 0)
    relay_x(3, 0)
    send_swap(0)
    relay_late(3)
    relay_x(0, 1)
    send_swap(1)
    send_swap(3)
    relay_x(1, 1)
    relay_last(3)
    send_swap(2)
    relay_x(2, 1)

    top = jnp.full((8, ROWS), -jnp.inf, F32)
    for k in FORTH:
        swap[k].wait_recv()
        for h in range(2):
            kb = kv[k, 0, h].reshape(256, HD)
            s = nt(kb, q_ref[...])
            scores[k, pl.ds(h * 256, 256)] = s
            top = jnp.maximum(top, jnp.max(s.reshape(32, 8, ROWS), axis=0))
    shift = jnp.max(top, axis=0, keepdims=True) * (FACTOR * LOG2E)
    total = jnp.zeros((8, ROWS), F32)
    acc_t = jnp.zeros((HD, ROWS), F32)
    for k in FORTH:
        for h in range(2):
            vb = kv[k, 1, h].reshape(256, HD)
            e = jnp.exp2(scores[k, pl.ds(h * 256, 256)] * (FACTOR * LOG2E) - shift)
            total = total + jnp.sum(e.reshape(32, 8, ROWS), axis=0)
            eb = e.astype(BF16)
            probs[k, pl.ds(h * 256, 256)] = eb
            acc_t = acc_t + tn(vb, eb)
    inverse = 1.0 / jnp.sum(total, axis=0, keepdims=True)
    att_t[...] = (acc_t * inverse).astype(BF16)

    for part in range(PARTS):
        for i in range(7):
            arrived(i, part)
    x_t = jnp.zeros((HD, ROWS), F32)
    for b in range(8):
        x_t = x_t + nt(w_ref[:, b * 128 : (b + 1) * 128], gall[b])
    x_t = x_t * inverse
    delta = jnp.sum(x_t * att_t[...].astype(F32), axis=0, keepdims=True)
    da_t[...] = x_t.astype(BF16)
    da[...] = x_t.T.astype(BF16)

    for b in range(8):
        part_w = nn(att_t[...], gall[b]).T
        for j in range(8):
            back, o = (z - (2 * b + j // 4) + 16) % 16, j % 4
            i = back % 4
            k = ((back + i // 3) // 4) % 4
            spot = acc.at[k, (core + o % 2) % 2, (yl + o // 2) % 2, i]
            spot[pl.ds(2 * KEYS, 16)] = part_w[j * 16 : (j + 1) * 16]

    dq_t[...] = jnp.zeros((HD, ROWS), F32)
    first, merged, last = {}, {}, {}

    def compute(k):
        for h in range(2):
            kb = kv[k, 0, h].reshape(256, HD)
            vb = kv[k, 1, h].reshape(256, HD)
            pb = probs[k, pl.ds(h * 256, 256)]
            ds = (pb.astype(F32) * (nn(vb, da_t[...]) - delta)).astype(BF16)
            acc[k, h, :, :, pl.ds(0, KEYS)] = (nn(ds, q_ref[...]) * FACTOR).reshape(2, 4, KEYS, HD)
            acc[k, h, :, :, pl.ds(KEYS, KEYS)] = nn(pb, da[...]).reshape(2, 4, KEYS, HD)
            dq_t[...] += tn(kb, ds)
        s1[k] = acc[k, 1].astype(BF16)
        first[k] = go(copy(s1.at[k], r1.at[k], c1_s.at[k], c1_r.at[k], on_ctx(dc=1)))

    def spread(k):
        first[k].wait_recv()
        for e, i in SPOTS:
            s3[k, e, i] = (acc[k, 0, e, i] + r1[k, e, i].astype(F32)).astype(BF16)
            merged[k, e, i] = go(
                copy(
                    s3.at[k, e, i],
                    r3.at[k, e, i],
                    m_s.at[k, e, i],
                    m_r.at[k, e, i],
                    on_ctx(dz=16 - NEAR[i], dy=e),
                )
            )

    def collect(k):
        total = acc[k, 0, 0, 0] + r1[k, 0, 0].astype(F32)
        for e, i in SPOTS:
            merged[k, e, i].wait_recv()
            total = total + r3[k, e, i].astype(F32)
        if k:
            s4[k] = total.astype(BF16)
            last[k] = go(copy(s4.at[k], r4.at[k], z4_s.at[k], z4_r.at[k], on_ctx(dz=16 - 4 * k)))
        return total

    compute(2)
    compute(1)
    spread(2)
    compute(3)
    spread(1)
    compute(0)
    spread(3)
    collect(2)
    spread(0)
    collect(1)
    collect(3)
    dq_ref[...] = (dq_t[...] * FACTOR).T.astype(BF16)
    mine = collect(0)
    for k in (1, 3, 2):
        last[k].wait_recv()
        mine = mine + r4[k].astype(F32)
    dk_ref[...] = mine[0:KEYS].astype(BF16)
    dv_ref[...] = mine[KEYS : 2 * KEYS].astype(BF16)
    dw_ref[...] = mine[2 * KEYS : SLOT]
    for c in sends:
        c.wait_send()


def local(queries, audio_keys, audio_values, grad_output, out_weight):
    vmem = pl.BlockSpec(memory_space=pltpu.VMEM)
    anywhere = pl.BlockSpec(memory_space=pl.ANY)
    dma = lambda *n: pltpu.SemaphoreType.DMA(n)
    scratch = [
        pltpu.VMEM((ROWS, HD), BF16),
        pltpu.VMEM((HD, 8 * HD), BF16),
        pltpu.VMEM((4, 2, 2, 2, 4, KEYS, HD), BF16),
        pltpu.VMEM((8, ROWS, 128), BF16),
        pltpu.VMEM((4, CHUNK, ROWS), F32),
        pltpu.VMEM((4, CHUNK, ROWS), BF16),
        pltpu.VMEM((HD, ROWS), BF16),
        pltpu.VMEM((HD, ROWS), BF16),
        pltpu.VMEM((ROWS, HD), BF16),
        pltpu.VMEM((HD, ROWS), F32),
        pltpu.VMEM((4, 2, 2, 4, SLOT, HD), F32),
        pltpu.VMEM((4, 2, 4, SLOT, HD), BF16),
        pltpu.VMEM((4, 2, 4, SLOT, HD), BF16),
        pltpu.VMEM((4, 2, 4, SLOT, HD), BF16),
        pltpu.VMEM((4, 2, 4, SLOT, HD), BF16),
        pltpu.VMEM((4, SLOT, HD), BF16),
        pltpu.VMEM((4, SLOT, HD), BF16),
        dma(5), dma(4), dma(4), dma(4, 2, 4), dma(4, 2, 4), dma(4), dma(4), dma(7, PARTS), dma(7, PARTS),
        dma(4), dma(4), dma(4, 2, 4), dma(4, 2, 4), dma(4), dma(4),
    ]
    shapes = (
        jax.ShapeDtypeStruct((ROWS, HD), BF16),
        jax.ShapeDtypeStruct((32, HD), BF16),
        jax.ShapeDtypeStruct((32, HD), BF16),
        jax.ShapeDtypeStruct((16, HD), F32),
    )
    dq, dk, dv, dw = pl.pallas_call(
        kernel,
        out_shape=shapes,
        in_specs=[anywhere] * 5,
        out_specs=(vmem,) * 4,
        scratch_shapes=scratch,
        compiler_params=pltpu.CompilerParams(
            collective_id=0, has_side_effects=True, vmem_limit_bytes=56 * 2**20
        ),
    )(queries, audio_keys, audio_values, grad_output, out_weight)
    return dq, dk, dv, dw.T


def solution(mesh):
    return jax.shard_map(
        local,
        mesh=mesh,
        in_specs=(P("ctx", "tp"), P("ctx", "tp"), P("ctx", "tp"), P("ctx", "tp"), P("tp", None)),
        out_specs=(P("ctx", "tp"), P("ctx", "tp"), P("ctx", "tp"), P("tp", "ctx")),
        check_vma=False,
    )
```

```python
import math

import jax
import jax.numpy as jnp
from jax import lax
from jax.experimental import pallas as pl
from jax.experimental.pallas import tpu as pltpu
from jax.sharding import PartitionSpec as P

MESH = pl.DeviceIdType.MESH
F32, BF16 = jnp.float32, jnp.bfloat16
HD = 128
ROWS = 1024
CHUNK = 512
KEYS = 32
SLOT = 80
PARTS = 4
PART = ROWS // PARTS
FACTOR = 1.0 / math.sqrt(HD)
LOG2E = math.log2(math.e)
NEAR = ((0, 1, 2, 15), (0, 1, 14, 15))
FORTH = (0, 1, 3, 2)
BACK = (2, 1, 3, 0)
PART_ORDER = (0, 1, 2, 3)
SPOTS = [(e, i) for i in (2, 1, 3, 0) for e in range(2) if i or e]


def nn(a, b):
    return lax.dot_general(a, b, (((1,), (0,)), ((), ())), preferred_element_type=F32)


def nt(a, b):
    return lax.dot_general(a, b, (((1,), (1,)), ((), ())), preferred_element_type=F32)


def tn(a, b):
    return lax.dot_general(a, b, (((0,), (0,)), ((), ())), preferred_element_type=F32)


def kernel(
    q_hbm, k_hbm, v_hbm, g_hbm, w_hbm,
    dq_hbm, dk_hbm, dv_hbm, dw_hbm,
    q_ref, w_ref, kv, gall, scores, probs, att_t, da_t, da, dq_t, acc,
    s1, r1, s3, r3, s4, r4, gw, delta_ref, dq_ref, dk_ref, dv_ref, dw_ref, out_s,
    in_s, far_s, far_r, near_s, near_r, ca_s, ca_r, g_s, g_r,
    c1_s, c1_r, m_s, m_r, z4_s, z4_r,
):
    ctx, tp = lax.axis_index("ctx"), lax.axis_index("tp")
    z, yl, core = ctx // 4, (ctx // 2) % 2, ctx % 2

    def on_ctx(dz=0, dy=0, dc=0):
        there = ((z + dz) % 16) * 4 + ((yl + dy) % 2) * 2 + (core + dc) % 2
        return (there, tp)

    def on_tp(dx, dy):
        return (ctx, ((tp // 2 + dx) % 4) * 2 + (tp % 2 + dy) % 2)

    def copy(src, dst, ssem, rsem, to):
        return pltpu.make_async_remote_copy(
            src_ref=src, dst_ref=dst, send_sem=ssem, recv_sem=rsem, device_id=to, device_id_type=MESH
        )

    own = kv.at[0, :, 0, 0, 0]
    loads = [
        pltpu.make_async_copy(k_hbm, own.at[0], in_s.at[0]),
        pltpu.make_async_copy(v_hbm, own.at[1], in_s.at[1]),
        pltpu.make_async_copy(g_hbm, gall.at[tp], in_s.at[2]),
        pltpu.make_async_copy(q_hbm, q_ref, in_s.at[3]),
        pltpu.make_async_copy(w_hbm, w_ref, in_s.at[4]),
    ]
    for c in loads:
        c.start()
    barrier = pltpu.get_barrier_semaphore()
    greeted = [on_ctx(dc=1), on_ctx(dy=1)]
    greeted += [on_ctx(dz=d, dy=e) for d in (1, 15, 2, 14) for e in range(2)]
    greeted += [on_ctx(dz=4), on_ctx(dz=12)]
    greeted += [on_tp(0, 1), on_tp(1, 0), on_tp(3, 0)]
    for there in greeted:
        pl.semaphore_signal(barrier, inc=1, device_id=there, device_id_type=MESH)
    for c in loads:
        c.wait()
    pl.semaphore_wait(barrier, len(greeted))

    sends = []

    def go(c):
        c.start()
        sends.append(c)
        return c

    far = {}

    def send_far(k, src, dz):
        far[k] = go(copy(src, kv.at[k, :, 0, 0, 0], far_s.at[k], far_r.at[k], on_ctx(dz=dz)))

    send_far(1, own, 4)
    send_far(3, own, 12)
    near = {}

    def send_near(k):
        if k:
            far[k].wait_recv()
        if k == 1:
            send_far(2, kv.at[1, :, 0, 0, 0], 4)
        for e, i in SPOTS:
            near[k, e, i] = go(
                copy(
                    kv.at[k, :, 0, 0, 0],
                    kv.at[k, :, 0, e, i],
                    near_s.at[k, e, i],
                    near_r.at[k, e, i],
                    on_ctx(dz=NEAR[e][i], dy=e),
                )
            )

    swap = {}

    def send_swap(k):
        for e, i in SPOTS:
            near[k, e, i].wait_recv()
        swap[k] = go(copy(kv.at[k, :, 0], kv.at[k, :, 1], ca_s.at[k], ca_r.at[k], on_ctx(dc=1)))

    send_near(0)

    gc = {}

    def send_grad(i, part, dx_from, dy_from, dx, dy):
        rows = pl.ds(part * PART, PART)
        b = gall.at[((tp // 2 + dx_from) % 4) * 2 + (tp % 2 + dy_from) % 2, rows]
        gc[i, part] = go(copy(b, b, g_s.at[i, part], g_r.at[i, part], on_tp(dx, dy)))

    waited = set()

    def arrived(i, part):
        if (i, part) not in waited:
            gc[i, part].wait_recv()
            waited.add((i, part))

    def relay_y(part):
        arrived(0, part)
        send_grad(3, part, 0, 1, 1, 0)
        send_grad(4, part, 0, 1, 3, 0)

    def relay_x(part, dy):
        if part % 2 == 0:
            arrived(1 + 2 * dy, part)
            send_grad(5 + dy, part, 3, dy, 1, 0)
        else:
            arrived(2 + 2 * dy, part)
            send_grad(5 + dy, part, 1, dy, 3, 0)

    def relay_late(part):
        arrived(1, part)
        send_grad(3, part, 3, 0, 0, 1)
        arrived(2, part)
        send_grad(4, part, 1, 0, 0, 1)

    def relay_last(part):
        arrived(5, part)
        send_grad(6, part, 2, 0, 0, 1)

    for part in range(PARTS):
        send_grad(0, part, 0, 0, 0, 1)
        send_grad(1, part, 0, 0, 1, 0)
        send_grad(2, part, 0, 0, 3, 0)
    relay_y(0)
    send_near(1)
    send_near(3)
    relay_y(1)
    relay_x(0, 0)
    relay_y(2)
    relay_x(1, 0)
    send_near(2)
    relay_x(2, 0)
    relay_x(3, 0)
    send_swap(0)
    relay_late(3)
    relay_x(0, 1)
    send_swap(1)
    send_swap(3)
    relay_x(1, 1)
    relay_last(3)
    send_swap(2)
    relay_x(2, 1)

    top = jnp.full((8, ROWS), -jnp.inf, F32)
    for k in FORTH:
        swap[k].wait_recv()
        for h in range(2):
            kb = kv[k, 0, h].reshape(256, HD)
            s = nt(kb, q_ref[...])
            scores[k, pl.ds(h * 256, 256)] = s
            top = jnp.maximum(top, jnp.max(s.reshape(32, 8, ROWS), axis=0))
    shift = jnp.max(top, axis=0, keepdims=True) * (FACTOR * LOG2E)
    total = jnp.zeros((8, ROWS), F32)
    acc_t = jnp.zeros((HD, ROWS), F32)
    for k in FORTH:
        for h in range(2):
            vb = kv[k, 1, h].reshape(256, HD)
            e = jnp.exp2(scores[k, pl.ds(h * 256, 256)] * (FACTOR * LOG2E) - shift)
            total = total + jnp.sum(e.reshape(32, 8, ROWS), axis=0)
            eb = e.astype(BF16)
            probs[k, pl.ds(h * 256, 256)] = eb
            acc_t = acc_t + tn(vb, eb)
    inverse = 1.0 / jnp.sum(total, axis=0, keepdims=True)
    att_t[...] = (acc_t * inverse).astype(BF16)

    for part in PART_ORDER:
        for i in range(7):
            arrived(i, part)
        rows = pl.ds(part * PART, PART)
        x_t = jnp.zeros((HD, PART), F32)
        for b in range(8):
            x_t = x_t + nt(w_ref[:, b * 128 : (b + 1) * 128], gall[b, rows])
            term = nn(att_t[:, rows], gall[b, rows])
            if part == PART_ORDER[0]:
                gw[b] = term
            else:
                gw[b] += term
        x_t = x_t * inverse[:, part * PART : (part + 1) * PART]
        delta_ref[:, rows] = jnp.sum(x_t * att_t[:, rows].astype(F32), axis=0, keepdims=True)
        da_t[:, rows] = x_t.astype(BF16)
        da[rows] = x_t.T.astype(BF16)
    delta = delta_ref[...]
    for b in range(8):
        part_w = gw[b].T
        for j in range(8):
            back, o = (z - (2 * b + j // 4) + 16) % 16, j % 4
            i, e = back % 4, (yl + o // 2) % 2
            k = ((back + i // 3 + 2 * e * (i // 2 - i // 3)) // 4) % 4
            spot = acc.at[k, (core + o % 2) % 2, e, i]
            spot[pl.ds(2 * KEYS, 16)] = part_w[j * 16 : (j + 1) * 16]

    dq_t[...] = jnp.zeros((HD, ROWS), F32)
    first, merged, last = {}, {}, {}

    def compute(k):
        for h in range(2):
            kb = kv[k, 0, h].reshape(256, HD)
            vb = kv[k, 1, h].reshape(256, HD)
            pb = probs[k, pl.ds(h * 256, 256)]
            ds = (pb.astype(F32) * (nn(vb, da_t[...]) - delta)).astype(BF16)
            acc[k, h, :, :, pl.ds(0, KEYS)] = (nn(ds, q_ref[...]) * FACTOR).reshape(2, 4, KEYS, HD)
            acc[k, h, :, :, pl.ds(KEYS, KEYS)] = nn(pb, da[...]).reshape(2, 4, KEYS, HD)
            dq_t[...] += tn(kb, ds)
        s1[k] = acc[k, 1].astype(BF16)
        first[k] = go(copy(s1.at[k], r1.at[k], c1_s.at[k], c1_r.at[k], on_ctx(dc=1)))

    def spread(k):
        first[k].wait_recv()
        for e, i in SPOTS:
            s3[k, e, i] = (acc[k, 0, e, i] + r1[k, e, i].astype(F32)).astype(BF16)
            merged[k, e, i] = go(
                copy(
                    s3.at[k, e, i],
                    r3.at[k, e, i],
                    m_s.at[k, e, i],
                    m_r.at[k, e, i],
                    on_ctx(dz=16 - NEAR[e][i], dy=e),
                )
            )

    def collect(k):
        total = acc[k, 0, 0, 0] + r1[k, 0, 0].astype(F32)
        for e, i in SPOTS:
            merged[k, e, i].wait_recv()
            total = total + r3[k, e, i].astype(F32)
        if k == 1:
            last[2].wait_recv()
            total = total + r4[2].astype(F32)
        if k:
            s4[k] = total.astype(BF16)
            there = on_ctx(dz=4 if k == 3 else 12)
            last[k] = go(copy(s4.at[k], r4.at[k], z4_s.at[k], z4_r.at[k], there))
        return total

    compute(2)
    compute(1)
    spread(2)
    compute(3)
    spread(1)
    compute(0)
    spread(3)
    collect(2)
    spread(0)
    collect(3)
    dq_ref[...] = (dq_t[...] * FACTOR).T.astype(BF16)
    results = [
        pltpu.make_async_copy(a, b, out_s.at[i])
        for i, (a, b) in enumerate(
            ((dq_ref, dq_hbm), (dk_ref, dk_hbm), (dv_ref, dv_hbm), (dw_ref, dw_hbm))
        )
    ]
    results[0].start()
    collect(1)
    mine = collect(0)
    for k in (3, 1):
        last[k].wait_recv()
        mine = mine + r4[k].astype(F32)
    dk_ref[...] = mine[0:KEYS].astype(BF16)
    dv_ref[...] = mine[KEYS : 2 * KEYS].astype(BF16)
    dw_ref[...] = mine[2 * KEYS : SLOT]
    for c in results[1:]:
        c.start()
    for c in sends:
        c.wait_send()
    for c in results:
        c.wait()


def finish(*refs):
    n = (len(refs) - 2) // 3
    ins, outs, held = refs[:n], refs[n : 2 * n], refs[2 * n : 3 * n]
    came, went = refs[3 * n :]
    first = [pltpu.make_async_copy(ins[i], held[i], came.at[i]) for i in range(n)]
    second = [pltpu.make_async_copy(held[i], outs[i], went.at[i]) for i in range(n)]
    for c in first:
        c.start()
    for a, b in zip(first, second):
        a.wait()
        b.start()
    for c in second:
        c.wait()


def local(queries, audio_keys, audio_values, grad_output, out_weight):
    anywhere = pl.BlockSpec(memory_space=pl.ANY)
    dma = lambda *n: pltpu.SemaphoreType.DMA(n)
    scratch = [
        pltpu.VMEM((ROWS, HD), BF16),
        pltpu.VMEM((HD, 8 * HD), BF16),
        pltpu.VMEM((4, 2, 2, 2, 4, KEYS, HD), BF16),
        pltpu.VMEM((8, ROWS, 128), BF16),
        pltpu.VMEM((4, CHUNK, ROWS), F32),
        pltpu.VMEM((4, CHUNK, ROWS), BF16),
        pltpu.VMEM((HD, ROWS), BF16),
        pltpu.VMEM((HD, ROWS), BF16),
        pltpu.VMEM((ROWS, HD), BF16),
        pltpu.VMEM((HD, ROWS), F32),
        pltpu.VMEM((4, 2, 2, 4, SLOT, HD), F32),
        pltpu.VMEM((4, 2, 4, SLOT, HD), BF16),
        pltpu.VMEM((4, 2, 4, SLOT, HD), BF16),
        pltpu.VMEM((4, 2, 4, SLOT, HD), BF16),
        pltpu.VMEM((4, 2, 4, SLOT, HD), BF16),
        pltpu.VMEM((4, SLOT, HD), BF16),
        pltpu.VMEM((4, SLOT, HD), BF16),
        pltpu.VMEM((8, HD, HD), F32),
        pltpu.VMEM((1, ROWS), F32),
        pltpu.VMEM((ROWS, HD), BF16),
        pltpu.VMEM((KEYS, HD), BF16),
        pltpu.VMEM((KEYS, HD), BF16),
        pltpu.VMEM((16, HD), F32),
        dma(4),
        dma(5), dma(4), dma(4), dma(4, 2, 4), dma(4, 2, 4), dma(4), dma(4), dma(7, PARTS), dma(7, PARTS),
        dma(4), dma(4), dma(4, 2, 4), dma(4, 2, 4), dma(4), dma(4),
    ]
    shapes = (
        jax.ShapeDtypeStruct((ROWS, HD), BF16),
        jax.ShapeDtypeStruct((32, HD), BF16),
        jax.ShapeDtypeStruct((32, HD), BF16),
        jax.ShapeDtypeStruct((16, HD), F32),
    )
    results = pl.pallas_call(
        kernel,
        out_shape=shapes,
        in_specs=[anywhere] * 5,
        out_specs=(anywhere,) * 4,
        scratch_shapes=scratch,
        compiler_params=pltpu.CompilerParams(
            collective_id=0, has_side_effects=True, vmem_limit_bytes=56 * 2**20
        ),
    )(queries, audio_keys, audio_values, grad_output, out_weight)
    dq, dk, dv, dw = pl.pallas_call(
        finish,
        out_shape=shapes,
        in_specs=[anywhere] * 4,
        out_specs=(anywhere,) * 4,
        scratch_shapes=[pltpu.VMEM(x.shape, x.dtype) for x in shapes] + [dma(4), dma(4)],
    )(*results)
    return dq, dk, dv, dw.T


def solution(mesh):
    return jax.shard_map(
        local,
        mesh=mesh,
        in_specs=(P("ctx", "tp"), P("ctx", "tp"), P("ctx", "tp"), P("ctx", "tp"), P("tp", None)),
        out_specs=(P("ctx", "tp"), P("ctx", "tp"), P("ctx", "tp"), P("tp", "ctx")),
        check_vma=False,
    )
```

```python
import math

import jax
import jax.numpy as jnp
from jax import lax
from jax.experimental import pallas as pl
from jax.experimental.pallas import tpu as pltpu
from jax.sharding import PartitionSpec as P

MESH = pl.DeviceIdType.MESH
F32, BF16 = jnp.float32, jnp.bfloat16
HD = 128
ROWS = 1024
CHUNK = 512
KEYS = 32
SLOT = 80
PARTS = 4
PART = ROWS // PARTS
FACTOR = 1.0 / math.sqrt(HD)
LOG2E = math.log2(math.e)
NEAR = ((0, 1, 2, 15), (0, 1, 14, 15))
FORTH = (0, 1, 3, 2)
BACK = (2, 1, 3, 0)
PART_ORDER = (0, 1, 2, 3)
SPOTS = [(e, i) for i in (2, 1, 3, 0) for e in range(2) if i or e]


def nn(a, b):
    return lax.dot_general(a, b, (((1,), (0,)), ((), ())), preferred_element_type=F32)


def nt(a, b):
    return lax.dot_general(a, b, (((1,), (1,)), ((), ())), preferred_element_type=F32)


def tn(a, b):
    return lax.dot_general(a, b, (((0,), (0,)), ((), ())), preferred_element_type=F32)


def kernel(
    q_hbm, k_hbm, v_hbm, g_hbm, w_hbm,
    dq_hbm, mine_hbm, got_hbm,
    q_ref, w_ref, kv, gall, scores, probs, att_t, da_t, da, dq_t, acc,
    s1, r1, s3, r3, s4, r4, gw, delta_ref, dq_ref, mine_ref, out_s,
    in_s, far_s, far_r, near_s, near_r, ca_s, ca_r, g_s, g_r,
    c1_s, c1_r, m_s, m_r, z4_s, z4_r,
):
    ctx, tp = lax.axis_index("ctx"), lax.axis_index("tp")
    z, yl, core = ctx // 4, (ctx // 2) % 2, ctx % 2

    def on_ctx(dz=0, dy=0, dc=0):
        there = ((z + dz) % 16) * 4 + ((yl + dy) % 2) * 2 + (core + dc) % 2
        return (there, tp)

    def on_tp(dx, dy):
        return (ctx, ((tp // 2 + dx) % 4) * 2 + (tp % 2 + dy) % 2)

    def copy(src, dst, ssem, rsem, to):
        return pltpu.make_async_remote_copy(
            src_ref=src, dst_ref=dst, send_sem=ssem, recv_sem=rsem, device_id=to, device_id_type=MESH
        )

    own = kv.at[0, :, 0, 0, 0]
    loads = [
        pltpu.make_async_copy(k_hbm, own.at[0], in_s.at[0]),
        pltpu.make_async_copy(v_hbm, own.at[1], in_s.at[1]),
        pltpu.make_async_copy(g_hbm, gall.at[tp], in_s.at[2]),
        pltpu.make_async_copy(q_hbm, q_ref, in_s.at[3]),
        pltpu.make_async_copy(w_hbm, w_ref, in_s.at[4]),
    ]
    for c in loads:
        c.start()
    barrier = pltpu.get_barrier_semaphore()
    greeted = [on_ctx(dc=1), on_ctx(dy=1)]
    greeted += [on_ctx(dz=d, dy=e) for d in (1, 15, 2, 14) for e in range(2)]
    greeted += [on_ctx(dz=4), on_ctx(dz=12)]
    greeted += [on_tp(0, 1), on_tp(1, 0), on_tp(3, 0)]
    for there in greeted:
        pl.semaphore_signal(barrier, inc=1, device_id=there, device_id_type=MESH)
    for c in loads:
        c.wait()
    pl.semaphore_wait(barrier, len(greeted))

    sends = []

    def go(c):
        c.start()
        sends.append(c)
        return c

    far = {}

    def send_far(k, src, dz):
        far[k] = go(copy(src, kv.at[k, :, 0, 0, 0], far_s.at[k], far_r.at[k], on_ctx(dz=dz)))

    send_far(1, own, 4)
    send_far(3, own, 12)
    near = {}

    def send_near(k):
        if k:
            far[k].wait_recv()
        if k == 1:
            send_far(2, kv.at[1, :, 0, 0, 0], 4)
        for e, i in SPOTS:
            near[k, e, i] = go(
                copy(
                    kv.at[k, :, 0, 0, 0],
                    kv.at[k, :, 0, e, i],
                    near_s.at[k, e, i],
                    near_r.at[k, e, i],
                    on_ctx(dz=NEAR[e][i], dy=e),
                )
            )

    swap = {}

    def send_swap(k):
        for e, i in SPOTS:
            near[k, e, i].wait_recv()
        swap[k] = go(copy(kv.at[k, :, 0], kv.at[k, :, 1], ca_s.at[k], ca_r.at[k], on_ctx(dc=1)))


    gc = {}

    def send_grad(i, part, dx_from, dy_from, dx, dy):
        rows = pl.ds(part * PART, PART)
        b = gall.at[((tp // 2 + dx_from) % 4) * 2 + (tp % 2 + dy_from) % 2, rows]
        gc[i, part] = go(copy(b, b, g_s.at[i, part], g_r.at[i, part], on_tp(dx, dy)))

    waited = set()

    def arrived(i, part):
        if (i, part) not in waited:
            gc[i, part].wait_recv()
            waited.add((i, part))

    def relay_y(part):
        arrived(0, part)
        send_grad(3, part, 0, 1, 1, 0)
        send_grad(4, part, 0, 1, 3, 0)

    def relay_x(part, dy):
        if part % 2 == 0:
            arrived(1 + 2 * dy, part)
            send_grad(5 + dy, part, 3, dy, 1, 0)
        else:
            arrived(2 + 2 * dy, part)
            send_grad(5 + dy, part, 1, dy, 3, 0)

    def relay_late(part):
        arrived(1, part)
        send_grad(3, part, 3, 0, 0, 1)
        arrived(2, part)
        send_grad(4, part, 1, 0, 0, 1)

    def relay_last(part):
        arrived(5, part)
        send_grad(6, part, 2, 0, 0, 1)

    for part in range(PARTS):
        send_grad(0, part, 0, 0, 0, 1)
        send_grad(1, part, 0, 0, 1, 0)
        send_grad(2, part, 0, 0, 3, 0)
    send_near(0)
    relay_y(0)
    send_near(1)
    send_near(3)
    relay_y(1)
    relay_x(0, 0)
    relay_y(2)
    relay_x(1, 0)
    send_near(2)
    relay_x(2, 0)
    relay_x(3, 0)
    send_swap(0)
    relay_late(3)
    relay_x(0, 1)
    send_swap(1)
    send_swap(3)
    relay_x(1, 1)
    relay_last(3)
    send_swap(2)
    relay_x(2, 1)

    top = jnp.full((8, ROWS), -jnp.inf, F32)
    for k in FORTH:
        swap[k].wait_recv()
        for h in range(2):
            kb = kv[k, 0, h].reshape(256, HD)
            s = nt(kb, q_ref[...])
            scores[k, pl.ds(h * 256, 256)] = s
            top = jnp.maximum(top, jnp.max(s.reshape(32, 8, ROWS), axis=0))
    shift = jnp.max(top, axis=0, keepdims=True) * (FACTOR * LOG2E)
    total = jnp.zeros((8, ROWS), F32)
    acc_t = jnp.zeros((HD, ROWS), F32)
    for k in FORTH:
        for h in range(2):
            vb = kv[k, 1, h].reshape(256, HD)
            e = jnp.exp2(scores[k, pl.ds(h * 256, 256)] * (FACTOR * LOG2E) - shift)
            total = total + jnp.sum(e.reshape(32, 8, ROWS), axis=0)
            eb = e.astype(BF16)
            probs[k, pl.ds(h * 256, 256)] = eb
            acc_t = acc_t + tn(vb, eb)
    inverse = 1.0 / jnp.sum(total, axis=0, keepdims=True)
    att_t[...] = (acc_t * inverse).astype(BF16)

    for part in PART_ORDER:
        for i in range(7):
            arrived(i, part)
        rows = pl.ds(part * PART, PART)
        x_t = jnp.zeros((HD, PART), F32)
        for b in range(8):
            x_t = x_t + nt(w_ref[:, b * 128 : (b + 1) * 128], gall[b, rows])
            term = nn(att_t[:, rows], gall[b, rows])
            if part == PART_ORDER[0]:
                gw[b] = term
            else:
                gw[b] += term
        x_t = x_t * inverse[:, part * PART : (part + 1) * PART]
        delta_ref[:, rows] = jnp.sum(x_t * att_t[:, rows].astype(F32), axis=0, keepdims=True)
        da_t[:, rows] = x_t.astype(BF16)
        da[rows] = x_t.T.astype(BF16)
    delta = delta_ref[...]
    for b in range(8):
        part_w = gw[b].T
        for j in range(8):
            back, o = (z - (2 * b + j // 4) + 16) % 16, j % 4
            i, e = back % 4, (yl + o // 2) % 2
            k = ((back + i // 3 + 2 * e * (i // 2 - i // 3)) // 4) % 4
            spot = acc.at[k, (core + o % 2) % 2, e, i]
            spot[pl.ds(2 * KEYS, 16)] = part_w[j * 16 : (j + 1) * 16]

    dq_t[...] = jnp.zeros((HD, ROWS), F32)
    first, merged, last = {}, {}, {}

    def compute(k):
        for h in range(2):
            kb = kv[k, 0, h].reshape(256, HD)
            vb = kv[k, 1, h].reshape(256, HD)
            pb = probs[k, pl.ds(h * 256, 256)]
            ds = (pb.astype(F32) * (nn(vb, da_t[...]) - delta)).astype(BF16)
            acc[k, h, :, :, pl.ds(0, KEYS)] = (nn(ds, q_ref[...]) * FACTOR).reshape(2, 4, KEYS, HD)
            acc[k, h, :, :, pl.ds(KEYS, KEYS)] = nn(pb, da[...]).reshape(2, 4, KEYS, HD)
            dq_t[...] += tn(kb, ds)
        s1[k] = acc[k, 1].astype(BF16)
        first[k] = go(copy(s1.at[k], r1.at[k], c1_s.at[k], c1_r.at[k], on_ctx(dc=1)))

    def spread(k):
        first[k].wait_recv()
        for e, i in SPOTS:
            s3[k, e, i] = (acc[k, 0, e, i] + r1[k, e, i].astype(F32)).astype(BF16)
            merged[k, e, i] = go(
                copy(
                    s3.at[k, e, i],
                    r3.at[k, e, i],
                    m_s.at[k, e, i],
                    m_r.at[k, e, i],
                    on_ctx(dz=16 - NEAR[e][i], dy=e),
                )
            )

    def collect(k):
        total = acc[k, 0, 0, 0] + r1[k, 0, 0].astype(F32)
        for e, i in SPOTS:
            merged[k, e, i].wait_recv()
            total = total + r3[k, e, i].astype(F32)
        if k == 1:
            last[2].wait_recv()
            total = total + r4[0].astype(F32)
        if k:
            s4[k] = total.astype(BF16)
            there = on_ctx(dz=4 if k == 3 else 12)
            lands = r4.at[0] if k == 2 else got_hbm.at[k // 2]
            last[k] = go(copy(s4.at[k], lands, z4_s.at[k], z4_r.at[k], there))
        return total

    compute(2)
    compute(1)
    spread(2)
    compute(3)
    spread(1)
    compute(0)
    spread(3)
    collect(2)
    spread(0)
    collect(3)
    dq_ref[...] = (dq_t[...] * FACTOR).T.astype(BF16)
    results = [
        pltpu.make_async_copy(dq_ref, dq_hbm, out_s.at[0]),
        pltpu.make_async_copy(mine_ref, mine_hbm, out_s.at[1]),
    ]
    results[0].start()
    collect(1)
    mine_ref[...] = collect(0)
    results[1].start()
    for k in (3, 1):
        last[k].wait_recv()
    for c in sends:
        c.wait_send()
    for c in results:
        c.wait()


def finish(dq_in, mine_in, got_in, dq_out, dk_out, dv_out, dw_out, dq, mine, got, dk, dv, dw, came, went):
    pieces = [pl.ds(i * PART, PART) for i in range(PARTS)]
    first = [
        pltpu.make_async_copy(mine_in, mine, came.at[0]),
        pltpu.make_async_copy(got_in, got, came.at[1]),
    ]
    first += [
        pltpu.make_async_copy(dq_in.at[rows], dq.at[rows], came.at[2 + i])
        for i, rows in enumerate(pieces)
    ]
    for c in first:
        c.start()
    second = [
        pltpu.make_async_copy(dk, dk_out, went.at[0]),
        pltpu.make_async_copy(dv, dv_out, went.at[1]),
        pltpu.make_async_copy(dw, dw_out, went.at[2]),
    ]
    second += [
        pltpu.make_async_copy(dq.at[rows], dq_out.at[rows], went.at[3 + i])
        for i, rows in enumerate(pieces)
    ]
    first[0].wait()
    first[1].wait()
    total = mine[...] + got[1].astype(F32) + got[0].astype(F32)
    dk[...] = total[0:KEYS].astype(BF16)
    dv[...] = total[KEYS : 2 * KEYS].astype(BF16)
    dw[...] = total[2 * KEYS : SLOT]
    for c in second[:3]:
        c.start()
    for i in range(PARTS):
        first[2 + i].wait()
        second[3 + i].start()
    for c in second:
        c.wait()


def local(queries, audio_keys, audio_values, grad_output, out_weight):
    anywhere = pl.BlockSpec(memory_space=pl.ANY)
    dma = lambda *n: pltpu.SemaphoreType.DMA(n)
    scratch = [
        pltpu.VMEM((ROWS, HD), BF16),
        pltpu.VMEM((HD, 8 * HD), BF16),
        pltpu.VMEM((4, 2, 2, 2, 4, KEYS, HD), BF16),
        pltpu.VMEM((8, ROWS, 128), BF16),
        pltpu.VMEM((4, CHUNK, ROWS), F32),
        pltpu.VMEM((4, CHUNK, ROWS), BF16),
        pltpu.VMEM((HD, ROWS), BF16),
        pltpu.VMEM((HD, ROWS), BF16),
        pltpu.VMEM((ROWS, HD), BF16),
        pltpu.VMEM((HD, ROWS), F32),
        pltpu.VMEM((4, 2, 2, 4, SLOT, HD), F32),
        pltpu.VMEM((4, 2, 4, SLOT, HD), BF16),
        pltpu.VMEM((4, 2, 4, SLOT, HD), BF16),
        pltpu.VMEM((4, 2, 4, SLOT, HD), BF16),
        pltpu.VMEM((4, 2, 4, SLOT, HD), BF16),
        pltpu.VMEM((4, SLOT, HD), BF16),
        pltpu.VMEM((1, SLOT, HD), BF16),
        pltpu.VMEM((8, HD, HD), F32),
        pltpu.VMEM((1, ROWS), F32),
        pltpu.VMEM((ROWS, HD), BF16),
        pltpu.VMEM((SLOT, HD), F32),
        dma(2),
        dma(5), dma(4), dma(4), dma(4, 2, 4), dma(4, 2, 4), dma(4), dma(4), dma(7, PARTS), dma(7, PARTS),
        dma(4), dma(4), dma(4, 2, 4), dma(4, 2, 4), dma(4), dma(4),
    ]
    shapes = (
        jax.ShapeDtypeStruct((ROWS, HD), BF16),
        jax.ShapeDtypeStruct((32, HD), BF16),
        jax.ShapeDtypeStruct((32, HD), BF16),
        jax.ShapeDtypeStruct((16, HD), F32),
    )
    parts = (
        shapes[0],
        jax.ShapeDtypeStruct((SLOT, HD), F32),
        jax.ShapeDtypeStruct((2, SLOT, HD), BF16),
    )
    results = pl.pallas_call(
        kernel,
        out_shape=parts,
        in_specs=[anywhere] * 5,
        out_specs=(anywhere,) * 3,
        scratch_shapes=scratch,
        compiler_params=pltpu.CompilerParams(
            collective_id=0, has_side_effects=True, vmem_limit_bytes=56 * 2**20
        ),
    )(queries, audio_keys, audio_values, grad_output, out_weight)
    dq, dk, dv, dw = pl.pallas_call(
        finish,
        out_shape=shapes,
        in_specs=[anywhere] * 3,
        out_specs=(anywhere,) * 4,
        scratch_shapes=[pltpu.VMEM(x.shape, x.dtype) for x in parts + shapes[1:]]
        + [dma(2 + PARTS), dma(3 + PARTS)],
    )(*results)
    return dq, dk, dv, dw.T


def solution(mesh):
    return jax.shard_map(
        local,
        mesh=mesh,
        in_specs=(P("ctx", "tp"), P("ctx", "tp"), P("ctx", "tp"), P("ctx", "tp"), P("tp", None)),
        out_specs=(P("ctx", "tp"), P("ctx", "tp"), P("ctx", "tp"), P("tp", "ctx")),
        check_vma=False,
    )
```

```python
import math

import jax
import jax.numpy as jnp
from jax import lax
from jax.experimental import pallas as pl
from jax.experimental.pallas import tpu as pltpu
from jax.sharding import PartitionSpec as P

MESH = pl.DeviceIdType.MESH
F32, BF16 = jnp.float32, jnp.bfloat16
HD = 128
ROWS = 1024
CHUNK = 512
KEYS = 32
SLOT = 80
PARTS = 4
PART = ROWS // PARTS
FACTOR = 1.0 / math.sqrt(HD)
LOG2E = math.log2(math.e)
NEAR = ((0, 1, 2, 15), (0, 1, 14, 15))
FORTH = (0, 1, 3, 2)
BACK = (2, 1, 3, 0)
PART_ORDER = (0, 1, 2, 3)
SPOTS = [(e, i) for i in (2, 1, 3, 0) for e in range(2) if i or e]


def nn(a, b):
    return lax.dot_general(a, b, (((1,), (0,)), ((), ())), preferred_element_type=F32)


def nt(a, b):
    return lax.dot_general(a, b, (((1,), (1,)), ((), ())), preferred_element_type=F32)


def tn(a, b):
    return lax.dot_general(a, b, (((0,), (0,)), ((), ())), preferred_element_type=F32)


def kernel(
    q_hbm, k_hbm, v_hbm, g_hbm, w_hbm,
    dq_hbm, mine_hbm, got_hbm,
    q_ref, w_ref, kv, gall, scores, probs, att_t, da_t, da, dq_t, acc,
    s1, r1, s3, r3, s4, r4, gw, delta_ref, dq_ref, mine_ref, out_s,
    in_s, far_s, far_r, near_s, near_r, ca_s, ca_r, g_s, g_r,
    c1_s, c1_r, m_s, m_r, z4_s, z4_r,
):
    ctx, tp = lax.axis_index("ctx"), lax.axis_index("tp")
    z, yl, core = ctx // 4, (ctx // 2) % 2, ctx % 2

    def on_ctx(dz=0, dy=0, dc=0):
        there = ((z + dz) % 16) * 4 + ((yl + dy) % 2) * 2 + (core + dc) % 2
        return (there, tp)

    def on_tp(dx, dy):
        return (ctx, ((tp // 2 + dx) % 4) * 2 + (tp % 2 + dy) % 2)

    def copy(src, dst, ssem, rsem, to):
        return pltpu.make_async_remote_copy(
            src_ref=src, dst_ref=dst, send_sem=ssem, recv_sem=rsem, device_id=to, device_id_type=MESH
        )

    own = kv.at[0, :, 0, 0, 0]
    loads = [
        pltpu.make_async_copy(k_hbm, own.at[0], in_s.at[0]),
        pltpu.make_async_copy(v_hbm, own.at[1], in_s.at[1]),
        pltpu.make_async_copy(g_hbm, gall.at[tp], in_s.at[2]),
        pltpu.make_async_copy(q_hbm, q_ref, in_s.at[3]),
        pltpu.make_async_copy(w_hbm, w_ref, in_s.at[4]),
    ]
    for c in loads:
        c.start()
    barrier = pltpu.get_barrier_semaphore()
    greeted = [on_ctx(dc=1), on_ctx(dy=1)]
    greeted += [on_ctx(dz=d, dy=e) for d in (1, 15, 2, 14) for e in range(2)]
    greeted += [on_ctx(dz=4), on_ctx(dz=12)]
    greeted += [on_tp(0, 1), on_tp(1, 0), on_tp(3, 0)]
    for there in greeted:
        pl.semaphore_signal(barrier, inc=1, device_id=there, device_id_type=MESH)
    for c in loads:
        c.wait()
    pl.semaphore_wait(barrier, len(greeted))

    sends = []

    def go(c):
        c.start()
        sends.append(c)
        return c

    far = {}

    def send_far(k, src, dz):
        far[k] = go(copy(src, kv.at[k, :, 0, 0, 0], far_s.at[k], far_r.at[k], on_ctx(dz=dz)))

    send_far(1, own, 4)
    send_far(3, own, 12)
    near = {}

    def send_near(k):
        if k:
            far[k].wait_recv()
        if k == 1:
            send_far(2, kv.at[1, :, 0, 0, 0], 4)
        for e, i in SPOTS:
            near[k, e, i] = go(
                copy(
                    kv.at[k, :, 0, 0, 0],
                    kv.at[k, :, 0, e, i],
                    near_s.at[k, e, i],
                    near_r.at[k, e, i],
                    on_ctx(dz=NEAR[e][i], dy=e),
                )
            )

    swap = {}

    def send_swap(k):
        for e, i in SPOTS:
            near[k, e, i].wait_recv()
        swap[k] = go(copy(kv.at[k, :, 0], kv.at[k, :, 1], ca_s.at[k], ca_r.at[k], on_ctx(dc=1)))


    gc = {}

    def send_grad(i, part, dx_from, dy_from, dx, dy):
        rows = pl.ds(part * PART, PART)
        b = gall.at[((tp // 2 + dx_from) % 4) * 2 + (tp % 2 + dy_from) % 2, rows]
        gc[i, part] = go(copy(b, b, g_s.at[i, part], g_r.at[i, part], on_tp(dx, dy)))

    waited = set()

    def arrived(i, part):
        if (i, part) not in waited:
            gc[i, part].wait_recv()
            waited.add((i, part))

    def relay_y(part):
        arrived(0, part)
        send_grad(3, part, 0, 1, 1, 0)
        send_grad(4, part, 0, 1, 3, 0)

    def relay_x(part, dy):
        if part % 2 == 0:
            arrived(1 + 2 * dy, part)
            send_grad(5 + dy, part, 3, dy, 1, 0)
        else:
            arrived(2 + 2 * dy, part)
            send_grad(5 + dy, part, 1, dy, 3, 0)

    def relay_late(part):
        arrived(1, part)
        send_grad(3, part, 3, 0, 0, 1)
        arrived(2, part)
        send_grad(4, part, 1, 0, 0, 1)

    def relay_last(part):
        arrived(5, part)
        send_grad(6, part, 2, 0, 0, 1)

    for part in range(PARTS):
        send_grad(0, part, 0, 0, 0, 1)
        send_grad(1, part, 0, 0, 1, 0)
        send_grad(2, part, 0, 0, 3, 0)
    send_near(0)
    send_near(1)
    relay_y(0)
    send_near(3)
    relay_y(1)
    relay_x(0, 0)
    relay_y(2)
    send_near(2)
    relay_x(1, 0)
    relay_x(2, 0)
    relay_x(3, 0)
    relay_late(3)
    send_swap(0)
    relay_x(0, 1)
    send_swap(1)
    relay_x(1, 1)
    send_swap(3)
    relay_last(3)
    relay_x(2, 1)
    send_swap(2)

    top = jnp.full((8, ROWS), -jnp.inf, F32)
    for k in FORTH:
        swap[k].wait_recv()
        for h in range(2):
            kb = kv[k, 0, h].reshape(256, HD)
            s = nt(kb, q_ref[...])
            scores[k, pl.ds(h * 256, 256)] = s
            top = jnp.maximum(top, jnp.max(s.reshape(32, 8, ROWS), axis=0))
    shift = jnp.max(top, axis=0, keepdims=True) * (FACTOR * LOG2E)
    total = jnp.zeros((8, ROWS), F32)
    acc_t = jnp.zeros((HD, ROWS), F32)
    for k in FORTH:
        for h in range(2):
            vb = kv[k, 1, h].reshape(256, HD)
            e = jnp.exp2(scores[k, pl.ds(h * 256, 256)] * (FACTOR * LOG2E) - shift)
            total = total + jnp.sum(e.reshape(32, 8, ROWS), axis=0)
            eb = e.astype(BF16)
            probs[k, pl.ds(h * 256, 256)] = eb
            acc_t = acc_t + tn(vb, eb)
    inverse = 1.0 / jnp.sum(total, axis=0, keepdims=True)
    att_t[...] = (acc_t * inverse).astype(BF16)

    for part in PART_ORDER:
        for i in range(7):
            arrived(i, part)
        rows = pl.ds(part * PART, PART)
        x_t = jnp.zeros((HD, PART), F32)
        for b in range(8):
            x_t = x_t + nt(w_ref[:, b * 128 : (b + 1) * 128], gall[b, rows])
            term = nn(att_t[:, rows], gall[b, rows])
            if part == PART_ORDER[0]:
                gw[b] = term
            else:
                gw[b] += term
        x_t = x_t * inverse[:, part * PART : (part + 1) * PART]
        delta_ref[:, rows] = jnp.sum(x_t * att_t[:, rows].astype(F32), axis=0, keepdims=True)
        da_t[:, rows] = x_t.astype(BF16)
        da[rows] = x_t.T.astype(BF16)
    delta = delta_ref[...]
    for b in range(8):
        part_w = gw[b].T
        for j in range(8):
            back, o = (z - (2 * b + j // 4) + 16) % 16, j % 4
            i, e = back % 4, (yl + o // 2) % 2
            k = ((back + i // 3 + 2 * e * (i // 2 - i // 3)) // 4) % 4
            spot = acc.at[k, (core + o % 2) % 2, e, i]
            spot[pl.ds(2 * KEYS, 16)] = part_w[j * 16 : (j + 1) * 16]

    dq_t[...] = jnp.zeros((HD, ROWS), F32)
    first, merged, last = {}, {}, {}

    def compute(k):
        held = []
        for h in range(2):
            kb = kv[k, 0, h].reshape(256, HD)
            vb = kv[k, 1, h].reshape(256, HD)
            pb = probs[k, pl.ds(h * 256, 256)]
            ds = (pb.astype(F32) * (nn(vb, da_t[...]) - delta)).astype(BF16)
            acc[k, h, :, :, pl.ds(0, KEYS)] = (nn(ds, q_ref[...]) * FACTOR).reshape(2, 4, KEYS, HD)
            acc[k, h, :, :, pl.ds(KEYS, KEYS)] = nn(pb, da[...]).reshape(2, 4, KEYS, HD)
            held.append((kb, ds))
        s1[k] = acc[k, 1].astype(BF16)
        first[k] = go(copy(s1.at[k], r1.at[k], c1_s.at[k], c1_r.at[k], on_ctx(dc=1)))
        for kb, ds in held:
            dq_t[...] += tn(kb, ds)

    def spread(k):
        first[k].wait_recv()
        for e, i in SPOTS:
            s3[k, e, i] = (acc[k, 0, e, i] + r1[k, e, i].astype(F32)).astype(BF16)
            merged[k, e, i] = go(
                copy(
                    s3.at[k, e, i],
                    r3.at[k, e, i],
                    m_s.at[k, e, i],
                    m_r.at[k, e, i],
                    on_ctx(dz=16 - NEAR[e][i], dy=e),
                )
            )

    def collect(k):
        total = acc[k, 0, 0, 0] + r1[k, 0, 0].astype(F32)
        for e, i in SPOTS:
            merged[k, e, i].wait_recv()
            total = total + r3[k, e, i].astype(F32)
        if k == 1:
            last[2].wait_recv()
            total = total + r4[0].astype(F32)
        if k:
            s4[k] = total.astype(BF16)
            there = on_ctx(dz=4 if k == 3 else 12)
            lands = r4.at[0] if k == 2 else got_hbm.at[k // 2]
            last[k] = go(copy(s4.at[k], lands, z4_s.at[k], z4_r.at[k], there))
        return total

    compute(2)
    compute(1)
    spread(2)
    compute(3)
    spread(1)
    compute(0)
    spread(3)
    collect(2)
    spread(0)
    collect(3)
    dq_ref[...] = (dq_t[...] * FACTOR).T.astype(BF16)
    results = [
        pltpu.make_async_copy(dq_ref, dq_hbm, out_s.at[0]),
        pltpu.make_async_copy(mine_ref, mine_hbm, out_s.at[1]),
    ]
    results[0].start()
    collect(1)
    mine_ref[...] = collect(0)
    results[1].start()
    for k in (3, 1):
        last[k].wait_recv()
    for c in sends:
        c.wait_send()
    for c in results:
        c.wait()


def finish(dq_in, mine_in, got_in, dq_out, dk_out, dv_out, dw_out, dq, mine, got, dk, dv, dw, came, went):
    pieces = [pl.ds(i * PART, PART) for i in range(PARTS)]
    first = [
        pltpu.make_async_copy(mine_in, mine, came.at[0]),
        pltpu.make_async_copy(got_in, got, came.at[1]),
    ]
    first += [
        pltpu.make_async_copy(dq_in.at[rows], dq.at[rows], came.at[2 + i])
        for i, rows in enumerate(pieces)
    ]
    for c in first:
        c.start()
    second = [
        pltpu.make_async_copy(dk, dk_out, went.at[0]),
        pltpu.make_async_copy(dv, dv_out, went.at[1]),
        pltpu.make_async_copy(dw, dw_out, went.at[2]),
    ]
    second += [
        pltpu.make_async_copy(dq.at[rows], dq_out.at[rows], went.at[3 + i])
        for i, rows in enumerate(pieces)
    ]
    first[0].wait()
    first[1].wait()
    total = mine[...] + got[1].astype(F32) + got[0].astype(F32)
    dk[...] = total[0:KEYS].astype(BF16)
    dv[...] = total[KEYS : 2 * KEYS].astype(BF16)
    dw[...] = total[2 * KEYS : SLOT]
    for c in second[:3]:
        c.start()
    for i in range(PARTS):
        first[2 + i].wait()
        second[3 + i].start()
    for c in second:
        c.wait()


def local(queries, audio_keys, audio_values, grad_output, out_weight):
    anywhere = pl.BlockSpec(memory_space=pl.ANY)
    dma = lambda *n: pltpu.SemaphoreType.DMA(n)
    scratch = [
        pltpu.VMEM((ROWS, HD), BF16),
        pltpu.VMEM((HD, 8 * HD), BF16),
        pltpu.VMEM((4, 2, 2, 2, 4, KEYS, HD), BF16),
        pltpu.VMEM((8, ROWS, 128), BF16),
        pltpu.VMEM((4, CHUNK, ROWS), F32),
        pltpu.VMEM((4, CHUNK, ROWS), BF16),
        pltpu.VMEM((HD, ROWS), BF16),
        pltpu.VMEM((HD, ROWS), BF16),
        pltpu.VMEM((ROWS, HD), BF16),
        pltpu.VMEM((HD, ROWS), F32),
        pltpu.VMEM((4, 2, 2, 4, SLOT, HD), F32),
        pltpu.VMEM((4, 2, 4, SLOT, HD), BF16),
        pltpu.VMEM((4, 2, 4, SLOT, HD), BF16),
        pltpu.VMEM((4, 2, 4, SLOT, HD), BF16),
        pltpu.VMEM((4, 2, 4, SLOT, HD), BF16),
        pltpu.VMEM((4, SLOT, HD), BF16),
        pltpu.VMEM((1, SLOT, HD), BF16),
        pltpu.VMEM((8, HD, HD), F32),
        pltpu.VMEM((1, ROWS), F32),
        pltpu.VMEM((ROWS, HD), BF16),
        pltpu.VMEM((SLOT, HD), F32),
        dma(2),
        dma(5), dma(4), dma(4), dma(4, 2, 4), dma(4, 2, 4), dma(4), dma(4), dma(7, PARTS), dma(7, PARTS),
        dma(4), dma(4), dma(4, 2, 4), dma(4, 2, 4), dma(4), dma(4),
    ]
    shapes = (
        jax.ShapeDtypeStruct((ROWS, HD), BF16),
        jax.ShapeDtypeStruct((32, HD), BF16),
        jax.ShapeDtypeStruct((32, HD), BF16),
        jax.ShapeDtypeStruct((16, HD), F32),
    )
    parts = (
        shapes[0],
        jax.ShapeDtypeStruct((SLOT, HD), F32),
        jax.ShapeDtypeStruct((2, SLOT, HD), BF16),
    )
    results = pl.pallas_call(
        kernel,
        out_shape=parts,
        in_specs=[anywhere] * 5,
        out_specs=(anywhere,) * 3,
        scratch_shapes=scratch,
        compiler_params=pltpu.CompilerParams(
            collective_id=0, has_side_effects=True, vmem_limit_bytes=56 * 2**20
        ),
    )(queries, audio_keys, audio_values, grad_output, out_weight)
    dq, dk, dv, dw = pl.pallas_call(
        finish,
        out_shape=shapes,
        in_specs=[anywhere] * 3,
        out_specs=(anywhere,) * 4,
        scratch_shapes=[pltpu.VMEM(x.shape, x.dtype) for x in parts + shapes[1:]]
        + [dma(2 + PARTS), dma(3 + PARTS)],
    )(*results)
    return dq, dk, dv, dw.T


def solution(mesh):
    return jax.shard_map(
        local,
        mesh=mesh,
        in_specs=(P("ctx", "tp"), P("ctx", "tp"), P("ctx", "tp"), P("ctx", "tp"), P("tp", None)),
        out_specs=(P("ctx", "tp"), P("ctx", "tp"), P("ctx", "tp"), P("tp", "ctx")),
        check_vma=False,
    )
```
